32 devices in a mesh: section: 2 (over x), tok: 4 (over z), mdl: 4 (over y, core).
Axes of the slice: x: 2, y: 2, z: 4, core: 2. Of those that a mesh axis runs over, the one named last changes fastest.
Arguments:
- layer_input: bfloat16 [2, 1024, 2048], P(None, 'tok'), may hold values from -6 to 6
- segment_ids: int32 [2, 1024], replicated, may hold values from 0 to 3, as said below
- route_ids: int32 [2, 1024, 6], P(None, ('tok', 'mdl')), may hold values from 0 to 15, all different within a row; in each aligned block of 64 rows (0 to 63, 64 to 127, ..., all dimensions but the last counted through in order) at most 36 rows name the same one
- route_weights: float32 [2, 1024, 6], P(None, ('tok', 'mdl')), may hold values from 0.1 to 0.5
- attn_gain: float32 [2048], replicated, may hold values from 0.5 to 1.5
- w_query: bfloat16 [2048, 3072], P(None, 'mdl'), may hold values from -6.629126 to 6.629126
- w_kv_down: bfloat16 [2048, 576], replicated, may hold values from -0.13258252 to 0.13258252
- latent_gain: float32 [512], replicated, may hold values from 0.5 to 1.5
- w_kv_up: bfloat16 [512, 4096], P(None, 'mdl'), may hold values from -0.25 to 0.25
- w_out: bfloat16 [2048, 2048], P('mdl'), may hold values from -0.125 to 0.125
- ffn_gain: float32 [2048], replicated, may hold values from 0.5 to 1.5
- w_shared_gate: bfloat16 [2048, 2048], P(None, 'mdl'), may hold values from -0.125 to 0.125
- w_shared_up: bfloat16 [2048, 2048], P(None, 'mdl'), may hold values from -0.125 to 0.125
- w_shared_down: bfloat16 [2048, 2048], P('mdl'), may hold values from -0.125 to 0.125
- w_expert_gate: bfloat16 [16, 2048, 768], P(('tok', 'mdl')), may hold values from -0.125 to 0.125
- w_expert_up: bfloat16 [16, 2048, 768], P(('tok', 'mdl')), may hold values from -0.125 to 0.125
- w_expert_down: bfloat16 [16, 768, 2048], P(('tok', 'mdl')), may hold values from -0.21875 to 0.21875
Outputs:
- layer_output: bfloat16 [2, 1024, 2048], P('section', ('tok', 'mdl'))
The draws below stay inside these ranges and needn't reach their ends.
Inputs may be any that keep to these rules, and one draw needn't show every extreme that they name: `segment_ids`: segment numbers never fall along a pack; each segment has 1 to 512 tokens and one has exactly 512. `route_ids`: each token names 6 different experts. In each aligned block of 64 tokens of a pack (the tokens of one device), no expert is named by more than 36 tokens, a bound that some block reaches.
All inputs are finite; a program needn't handle non-finite values.
Results may differ from the reference program's by a relative error of at most 0.02.
Values may be sent and summed in bfloat16 or wider, within the bound.
A program may use at most 128 MiB of HBM per device.

```python
import math
import jax
import jax.numpy as jnp
import numpy as np
from jax import lax

D = 2048
HEADS = 16
NOPE = 128
ROPE = 64
VDIM = 128
LATENT = 512
FFE = 768
SHARED = 2048
TOPK = 6
MICRO = 2
SEGS = 4
PACK = 1024
LONGEST = 512
R_DEV = 64
EXPERTS = 16
CAP = 36
BUF = 576


def common_direction(key):
    flips = jax.random.bernoulli(jax.random.fold_in(key, 91), 0.5, (D,))
    return jnp.where(flips, 1.0, -1.0).astype(jnp.float32)


def slow_pairs(key):
    half_width = ROPE // 2
    low_count = max(1, ROPE // 16)
    index_all = jnp.arange(ROPE, dtype=jnp.int32)
    pair_index = index_all % half_width
    flips = jax.random.bernoulli(jax.random.fold_in(key, 93), 0.5, (ROPE,))
    signs = jnp.where(flips, 1.0, -1.0).astype(jnp.float32)
    return jnp.where(pair_index >= half_width - low_count, signs, 0.0) / math.sqrt(2.0 * low_count)


def coupling_strength():
    return (100.0 * (NOPE + ROPE)) ** 0.25


def segment_layout(key):
    rest_tokens = PACK - LONGEST
    labels = jnp.arange(SEGS, dtype=jnp.int32)
    token_index = jnp.arange(PACK, dtype=jnp.int32)
    rows = []
    for batch_idx in range(MICRO):
        batch_key = jax.random.fold_in(key, 500 + batch_idx)
        shuffled = jax.random.permutation(jax.random.fold_in(batch_key, 1), rest_tokens - 1).astype(jnp.int32) + 1
        cuts = jnp.sort(shuffled[:SEGS - 2])
        bounds = jnp.concatenate([jnp.zeros((1,), jnp.int32), cuts, jnp.full((1,), rest_tokens, jnp.int32)])
        short_lengths = bounds[1:] - bounds[:-1]
        long_slot = jax.random.randint(jax.random.fold_in(batch_key, 2), (), 0, SEGS).astype(jnp.int32)
        before = jnp.clip(labels, 0, SEGS - 2)
        after = jnp.clip(labels - 1, 0, SEGS - 2)
        lengths = jnp.where(labels < long_slot, short_lengths[before], jnp.where(labels == long_slot, LONGEST, short_lengths[after])).astype(jnp.int32)
        starts = jnp.cumsum(lengths) - lengths
        ids = jnp.sum((token_index[:, None] >= starts[None, 1:]).astype(jnp.int32), axis=1)
        rows.append(ids)
    return jnp.stack(rows).astype(jnp.int32)


def draw_segment_ids(key, part):
    return segment_layout(key)


def draw_layer_input(key, part):
    segments = segment_layout(key)
    labels = jnp.arange(SEGS, dtype=jnp.int32)
    starts = jnp.sum((segments[:, None, :] < labels[None, :, None]).astype(jnp.int32), axis=2)
    first_rows = jnp.take_along_axis(starts, segments, axis=1)
    positions = jnp.arange(PACK, dtype=jnp.int32)[None, :] - first_rows
    opening = positions < 8
    noise = jnp.clip(jax.random.normal(jax.random.fold_in(key, 31), (MICRO, PACK, D), jnp.float32), -4.0, 4.0)
    strength = jnp.where(opening, 2.0, -0.5).astype(jnp.float32)
    rows = noise + strength[:, :, None] * common_direction(key)[None, None, :]
    return rows.astype(jnp.bfloat16)


def draw_w_query(key, part):
    base = jnp.clip(jax.random.normal(jax.random.fold_in(key, 13), (D, HEADS, NOPE + ROPE), jnp.float32), -5.0, 5.0) / math.sqrt(D)
    rope_cols = base[:, :, NOPE:]
    sink_term = coupling_strength() / D * common_direction(key)[:, None, None] * slow_pairs(key)[None, None, :]
    rope_cols = rope_cols - sink_term
    full = jnp.concatenate([base[:, :, :NOPE], rope_cols], axis=2)
    limit = 300.0 / math.sqrt(D)
    full = jnp.clip(full, -limit, limit)
    return full.reshape(D, HEADS * (NOPE + ROPE)).astype(jnp.bfloat16)


def draw_w_kv_down(key, part):
    base = jnp.clip(jax.random.normal(jax.random.fold_in(key, 11), (D, LATENT + ROPE), jnp.float32), -5.0, 5.0) / math.sqrt(D)
    rope_cols = base[:, LATENT:]
    sink_term = coupling_strength() / D * common_direction(key)[:, None] * slow_pairs(key)[None, :]
    rope_cols = rope_cols + sink_term
    return jnp.concatenate([base[:, :LATENT], rope_cols], axis=1).astype(jnp.bfloat16)


def steps_of(key, extent, split, low, high):
    level = 1.0
    for axis_at, blocks in split:
        steps = jax.random.uniform(jax.random.fold_in(jax.random.fold_in(key, 6), axis_at), (blocks,), jnp.float32, low / len(split), high / len(split))
        level = level * jnp.repeat(jnp.exp(steps), extent[axis_at] // blocks).reshape((-1,) + (1,) * (len(extent) - 1 - axis_at))
    return level


def deal_out(stream_key, own, number, rows, count, top, bound, slope):
    ranking = jax.random.permutation(stream_key, count)
    heavy_load, ordinary = load_shares(count, rows * top, bound, slope, True), load_shares(count, rows * top, bound, slope, False)
    places = jnp.arange(count)

    def named(sizes, rotation):
        used = int((sizes > 0).sum())
        fixed = max(1, used // 4)
        shifted = fixed + (places - fixed + rotation * (used - fixed)) % max(1, count - fixed)
        return jnp.zeros((count,), jnp.int32).at[ranking[jnp.where(places < fixed, places, shifted)]].set(jnp.asarray(sizes, jnp.int32))

    sizes = jnp.where(number % 4 == 0, named(heavy_load, number // 4), named(ordinary, number - number // 4 - 1))
    mixed = jax.random.permutation(jax.random.fold_in(own, 3), count)
    donor, taker = mixed[0:count // 2 * 2:2], mixed[1:count // 2 * 2:2]
    slack = jnp.minimum(sizes[donor] - 1, bound - sizes[taker]) // 2
    slack = jnp.where((donor == ranking[0]) | (taker == ranking[0]) | (sizes[taker] == 0), 0, jnp.maximum(slack, 0))
    shifted = jax.random.randint(jax.random.fold_in(own, 4), (count // 2,), 0, 1 << 20) % (slack + 1)
    sizes = sizes.at[donor].add(-shifted).at[taker].add(shifted)
    members = jnp.searchsorted(jnp.cumsum(sizes), jnp.arange(rows * top), side="right").astype(jnp.int32)
    listing = members.reshape(top, rows).T
    listing = listing[jax.random.permutation(jax.random.fold_in(own, 1), rows)]
    rotation = jax.random.randint(jax.random.fold_in(own, 2), (rows, 1), 0, top)
    return jnp.take_along_axis(listing, (jnp.arange(top)[None, :] + rotation) % top, axis=1)


def load_shares(amount, total, reach, skew, full):
    loads = [(1 << 20) // math.isqrt(standing ** skew) + 1 for standing in range(1, amount + 1)]
    largest = reach if full else min(reach, max(-(-total // amount), total * loads[0] // sum(loads)))
    least = 1 if total - largest >= amount - 1 else 0
    counts, rest = [largest] + [least] * (amount - 1), total - largest - least * (amount - 1)
    while rest > 0:
        candidates = [i for i in range(1, amount) if counts[i] < largest] or [i for i in range(1, amount) if counts[i] < reach]
        mass, remaining = sum([loads[i] for i in candidates]), rest
        for i in candidates:
            extra = min(reach - counts[i], max(1, remaining * loads[i] // mass), rest)
            counts[i] = counts[i] + extra
            rest = rest - extra
    return np.array(counts)


def centred(own_key, extent, deviation, most, split=(), kind=jnp.bfloat16):
    level = steps_of(own_key, extent, split, -0.22, 0.18) if split else 1.0
    array = jax.random.normal(own_key, extent, jnp.float32) * deviation * level
    return jnp.minimum(jnp.maximum(array, -most), most).astype(kind)


def setup_inputs(seed: int = 0) -> dict:
    streams_of = jax.random.split(jax.random.key(seed), 18)
    layer_input = draw_layer_input(jax.random.fold_in(streams_of[17], 71), 0)
    segment_ids = draw_segment_ids(jax.random.fold_in(streams_of[17], 71), 0)
    route_ids_keys = jax.random.split(jax.random.fold_in(streams_of[2], 1), MICRO * PACK // R_DEV)
    route_ids_turns = jax.random.permutation(jax.random.fold_in(streams_of[2], 3), MICRO * PACK // R_DEV)
    route_ids = jax.vmap(lambda own, number: deal_out(jax.random.fold_in(streams_of[2], 2), own, number, R_DEV, EXPERTS, TOPK, CAP, 2))(route_ids_keys, route_ids_turns).reshape((MICRO, PACK, TOPK))
    route_weights = jnp.clip(0.1 + 0.4 * jax.random.uniform(streams_of[3], (MICRO, PACK, TOPK), jnp.float32) ** steps_of(streams_of[3], (MICRO, PACK, TOPK), ((1, 16),), -0.2, 0.2), 0.1, 0.5)
    attn_gain = jnp.clip(1.0 + 0.1 * jax.random.normal(streams_of[4], (D,), jnp.float32), 0.5, 1.5)
    w_query = draw_w_query(jax.random.fold_in(streams_of[17], 71), 0)
    w_kv_down = draw_w_kv_down(jax.random.fold_in(streams_of[17], 71), 0)
    latent_gain = jnp.clip(1.0 + 0.1 * jax.random.normal(streams_of[7], (LATENT,), jnp.float32), 0.5, 1.5)
    w_kv_up = centred(streams_of[8], (LATENT, HEADS * (NOPE + VDIM)), LATENT ** -0.5, 0.25, ((1, 4),))
    w_out = centred(streams_of[9], (HEADS * VDIM, D), (HEADS * VDIM) ** -0.5, 0.125, ((0, 4),))
    ffn_gain = jnp.clip(1.0 + 0.1 * jax.random.normal(streams_of[10], (D,), jnp.float32), 0.5, 1.5)
    w_shared_gate = centred(streams_of[11], (D, SHARED), D ** -0.5, 0.125, ((1, 4),))
    w_shared_up = centred(streams_of[12], (D, SHARED), D ** -0.5, 0.125, ((1, 4),))
    w_shared_down = centred(streams_of[13], (SHARED, D), SHARED ** -0.5, 0.125, ((0, 4),))
    w_expert_gate = centred(streams_of[14], (EXPERTS, D, FFE), D ** -0.5, 0.125, ((0, 16),))
    w_expert_up = centred(streams_of[15], (EXPERTS, D, FFE), D ** -0.5, 0.125, ((0, 16),))
    w_expert_down = centred(streams_of[16], (EXPERTS, FFE, D), FFE ** -0.5, 0.21875, ((0, 16),))
    return {"layer_input": layer_input, "segment_ids": segment_ids, "route_ids": route_ids, "route_weights": route_weights, "attn_gain": attn_gain, "w_query": w_query, "w_kv_down": w_kv_down, "latent_gain": latent_gain, "w_kv_up": w_kv_up, "w_out": w_out, "ffn_gain": ffn_gain, "w_shared_gate": w_shared_gate, "w_shared_up": w_shared_up, "w_shared_down": w_shared_down, "w_expert_gate": w_expert_gate, "w_expert_up": w_expert_up, "w_expert_down": w_expert_down}


EPS = 1e-06

def rms_scale(values, gain_vec):
    values = values.astype(jnp.float32)
    return values * lax.rsqrt(lax.optimization_barrier(jnp.mean(values * values, axis=-1, keepdims=True)) + EPS) * gain_vec.astype(jnp.float32)

def rotary(values, positions):
    half_width = values.shape[-1] // 2
    frequency = 10000.0 ** (-jnp.arange(half_width, dtype=jnp.float32) / half_width)
    angles = positions.astype(jnp.float32)[:, None] * frequency[None, :]
    if values.ndim == 3:
        angles = angles[:, None, :]
    cosine = jnp.cos(angles)
    sine_part = jnp.sin(angles)
    lead_half = values[..., :half_width]
    tail_half = values[..., half_width:]
    return jnp.concatenate([lead_half * cosine - tail_half * sine_part, lead_half * sine_part + tail_half * cosine], axis=-1)

def attention_head(query_head, key_head, value_head, allowed, score_scale):
    scores = jnp.dot(query_head, key_head.T, preferred_element_type=jnp.float32) * score_scale
    masked = jnp.where(allowed, scores, -jnp.inf)
    running_max = lax.optimization_barrier(jnp.max(masked, axis=1, keepdims=True))
    weights = jnp.where(allowed, jnp.exp(scores - running_max), 0.0)
    totals = lax.optimization_barrier(jnp.sum(weights, axis=1, keepdims=True))
    summed = jnp.dot(weights.astype(jnp.bfloat16), value_head, preferred_element_type=jnp.float32)
    return (summed / totals).astype(jnp.bfloat16)

def one_batch(rows_in, segment_row, expert_ids, expert_weights, attn_gain, w_query, w_kv_down, latent_gain, w_kv_up, w_out, ffn_gain, w_shared_gate, w_shared_up, w_shared_down, w_expert_gate, w_expert_up, w_expert_down):
    labels = jnp.arange(SEGS, dtype=jnp.int32)
    starts = lax.optimization_barrier(jnp.sum((segment_row[None, :] < labels[:, None]).astype(jnp.int32), axis=1))
    token_index = jnp.arange(PACK, dtype=jnp.int32)
    positions = token_index - starts[segment_row]
    normed = rms_scale(rows_in, attn_gain).astype(jnp.bfloat16)
    queries = jnp.dot(normed, w_query, preferred_element_type=jnp.float32).reshape(PACK, HEADS, NOPE + ROPE)
    queries = jnp.concatenate([queries[..., :NOPE], rotary(queries[..., NOPE:], positions)], axis=-1).astype(jnp.bfloat16)
    compressed = jnp.dot(normed, w_kv_down, preferred_element_type=jnp.float32)
    latent = rms_scale(compressed[:, :LATENT], latent_gain).astype(jnp.bfloat16)
    key_rope = rotary(compressed[:, LATENT:], positions).astype(jnp.bfloat16)
    expanded = jnp.dot(latent, w_kv_up, preferred_element_type=jnp.float32).astype(jnp.bfloat16).reshape(PACK, HEADS, NOPE + VDIM)
    allowed = (segment_row[:, None] == segment_row[None, :]) & (token_index[None, :] <= token_index[:, None])
    score_scale = 1.0 / jnp.sqrt(jnp.float32(NOPE + ROPE))

    def per_head(head_inputs):
        query_head, nope_head, value_head = head_inputs
        key_head = jnp.concatenate([nope_head, key_rope], axis=-1)
        return attention_head(query_head, key_head, value_head, allowed, score_scale)
    heads_out = lax.map(per_head, (queries.transpose(1, 0, 2), expanded[..., :NOPE].transpose(1, 0, 2), expanded[..., NOPE:].transpose(1, 0, 2)))
    attended = heads_out.transpose(1, 0, 2).reshape(PACK, HEADS * VDIM)
    residual = (rows_in.astype(jnp.float32) + jnp.dot(attended, w_out, preferred_element_type=jnp.float32)).astype(jnp.bfloat16)
    normed_ffn = rms_scale(residual, ffn_gain).astype(jnp.bfloat16)
    shared_act = (jax.nn.silu(jnp.dot(normed_ffn, w_shared_gate, preferred_element_type=jnp.float32)) * jnp.dot(normed_ffn, w_shared_up, preferred_element_type=jnp.float32)).astype(jnp.bfloat16)
    shared_out = jnp.dot(shared_act, w_shared_down, preferred_element_type=jnp.float32)

    def expert_step(routed, expert):
        matched = expert_ids == expert
        row_weight = lax.optimization_barrier(jnp.sum(jnp.where(matched, expert_weights, 0.0), axis=1))
        chosen = jnp.any(matched, axis=1)
        chosen_count = jnp.sum(chosen.astype(jnp.int32))
        where_rows = jnp.nonzero(chosen, size=BUF, fill_value=0)[0].astype(jnp.int32)
        picked = normed_ffn[where_rows]
        gate_proj = jnp.dot(picked, w_expert_gate[expert], preferred_element_type=jnp.float32)
        up_proj = jnp.dot(picked, w_expert_up[expert], preferred_element_type=jnp.float32)
        expert_act = (jax.nn.silu(gate_proj) * up_proj).astype(jnp.bfloat16)
        expert_out = jnp.dot(expert_act, w_expert_down[expert], preferred_element_type=jnp.float32).astype(jnp.bfloat16)
        valid = jnp.arange(BUF, dtype=jnp.int32) < chosen_count
        scaling = jnp.where(valid, row_weight[where_rows], 0.0)
        routed = routed.at[where_rows].add(scaling[:, None] * expert_out.astype(jnp.float32))
        return (routed, None)
    routed, unused = lax.scan(expert_step, jnp.zeros((PACK, D), jnp.float32), jnp.arange(EXPERTS, dtype=jnp.int32))
    return (residual.astype(jnp.float32) + shared_out + routed).astype(jnp.bfloat16)

def reference(layer_input, segment_ids, route_ids, route_weights, attn_gain, w_query, w_kv_down, latent_gain, w_kv_up, w_out, ffn_gain, w_shared_gate, w_shared_up, w_shared_down, w_expert_gate, w_expert_up, w_expert_down):
    outputs = []
    for batch_idx in range(MICRO):
        outputs.append(one_batch(layer_input[batch_idx], segment_ids[batch_idx], route_ids[batch_idx], route_weights[batch_idx], attn_gain, w_query, w_kv_down, latent_gain, w_kv_up, w_out, ffn_gain, w_shared_gate, w_shared_up, w_shared_down, w_expert_gate, w_expert_up, w_expert_down))
    return jnp.stack(outputs)
```

```python
import functools
import math

import jax
import jax.numpy as jnp
from jax import lax
from jax.experimental import pallas as pl
from jax.experimental.pallas import tpu as pltpu
from jax.sharding import PartitionSpec as P

NOPE = 128
ROPE = 64
VDIM = 128
LATENT = 512
SEGS = 4
EPS = 1e-06
BF16 = jnp.bfloat16
F32 = jnp.float32


def rms_scale(values, gain_vec):
    values = values.astype(F32)
    return values * lax.rsqrt(jnp.mean(values * values, axis=-1, keepdims=True) + EPS) * gain_vec


def rotary_tables(positions):
    half_width = ROPE // 2
    frequency = 10000.0 ** (-jnp.arange(half_width, dtype=F32) / half_width)
    angles = positions.astype(F32)[:, None] * frequency[None, :]
    cosine = jnp.cos(angles)
    sine = jnp.sin(angles)
    return jnp.concatenate([cosine, cosine], axis=1), jnp.concatenate([-sine, sine], axis=1)


def turned(values, cosine, sine):
    half_width = values.shape[-1] // 2
    swapped = jnp.concatenate([values[:, half_width:], values[:, :half_width]], axis=1)
    return values * cosine + swapped * sine


def silu_mul(gate, up):
    return gate / (1.0 + jnp.exp(-gate)) * up


def attend_kernel(
    q_ref, lat_ref, kr_ref, wkv_ref, wo_ref, cos_ref, sin_ref, low_ref, high_ref, out_ref, att_ref
):
    heads = wo_ref.shape[0] // VDIM
    width = NOPE + ROPE
    span = lat_ref.shape[0]
    scale = 1.0 / math.sqrt(width)
    rope_keys = kr_ref[...]
    cosine, sine = cos_ref[...], sin_ref[...]
    key_index = lax.broadcasted_iota(jnp.int32, (q_ref.shape[0], span), 1)
    allowed = (key_index >= low_ref[...]) & (key_index <= high_ref[...])
    contract = (((1,), (1,)), ((), ()))
    for h in range(heads):
        kv = jnp.dot(
            lat_ref[...],
            wkv_ref[:, h * (NOPE + VDIM) : (h + 1) * (NOPE + VDIM)],
            preferred_element_type=F32,
        ).astype(BF16)
        q_nope = q_ref[:, h * width : h * width + NOPE].astype(BF16)
        q_rope = turned(q_ref[:, h * width + NOPE : (h + 1) * width], cosine, sine).astype(BF16)
        scores = lax.dot_general(q_nope, kv[:, :NOPE], contract, preferred_element_type=F32)
        scores += lax.dot_general(q_rope, rope_keys, contract, preferred_element_type=F32)
        scores = jnp.where(allowed, scores * scale, -1e30)
        top = jnp.max(scores, axis=1, keepdims=True)
        weights = jnp.where(allowed, jnp.exp(scores - top), 0.0)
        total = jnp.sum(weights, axis=1, keepdims=True)
        summed = jnp.dot(weights.astype(BF16), kv[:, NOPE:], preferred_element_type=F32)
        att_ref[:, h * VDIM : (h + 1) * VDIM] = (summed / total).astype(BF16)
    out_ref[...] = jnp.dot(att_ref[...], wo_ref[...], preferred_element_type=F32).astype(BF16)


def attend(queries, latent, rope_keys, w_kv_up, w_out, cosine, sine, low, high):
    rows = queries.shape[0]
    return pl.pallas_call(
        attend_kernel,
        out_shape=jax.ShapeDtypeStruct((rows, w_out.shape[1]), BF16),
        in_specs=[pl.BlockSpec(memory_space=pltpu.VMEM)] * 9,
        out_specs=pl.BlockSpec(memory_space=pltpu.VMEM),
        scratch_shapes=[pltpu.VMEM((rows, w_out.shape[0]), BF16)],
        compiler_params=pltpu.CompilerParams(vmem_limit_bytes=40 * 2**20),
        cost_estimate=pl.CostEstimate(
            flops=3 * 10**9, bytes_accessed=6 * 10**6, transcendentals=10**6
        ),
    )(queries, latent, rope_keys, w_kv_up, w_out, cosine, sine, low, high)


def shards(
    layer_input,
    segment_ids,
    route_ids,
    route_weights,
    attn_gain,
    w_query,
    w_kv_down,
    latent_gain,
    w_kv_up,
    w_out,
    ffn_gain,
    w_shared_gate,
    w_shared_up,
    w_shared_down,
    w_expert_gate,
    w_expert_up,
    w_expert_down,
):
    n_mdl = lax.axis_size("mdl")
    n_wide = lax.axis_size(("tok", "mdl"))
    section_id = lax.axis_index("section")
    tok_rank = lax.axis_index("tok")
    mdl_rank = lax.axis_index("mdl")
    micro_count, tok_dev, model_width = layer_input.shape
    per_section = micro_count // lax.axis_size("section")
    row_dev = tok_dev // n_mdl
    pack = segment_ids.shape[1]
    expert_dev = w_expert_gate.shape[0]
    expert_total = expert_dev * n_wide
    span = min(pack, pack // 2 + tok_dev)
    results = []
    for step in range(per_section):
        batch = section_id * per_section + step
        rows_in = lax.dynamic_index_in_dim(layer_input, batch, 0, keepdims=False)
        segment_row = lax.dynamic_index_in_dim(segment_ids, batch, 0, keepdims=False)
        chosen = lax.dynamic_index_in_dim(route_ids, batch, 0, keepdims=False)
        chosen_weights = lax.dynamic_index_in_dim(route_weights, batch, 0, keepdims=False)
        labels = jnp.arange(expert_total, dtype=jnp.int32)
        combining = jnp.sum(
            jnp.where(chosen[:, :, None] == labels, chosen_weights[:, :, None], 0.0), axis=1
        )
        all_combining = lax.all_gather(combining, ("tok", "mdl"), axis=0, tiled=True)

        query_start = tok_rank * tok_dev
        query_seg = lax.dynamic_slice_in_dim(segment_row, query_start, tok_dev)
        firsts = jnp.sum((segment_row[None, :] < query_seg[:, None]).astype(jnp.int32), axis=1)
        query_index = query_start + jnp.arange(tok_dev, dtype=jnp.int32)
        cosine, sine = rotary_tables(query_index - firsts)
        window = jnp.clip(query_start - pack // 2, 0, pack - span)
        low = (firsts - window)[:, None]
        high = (query_index - window)[:, None]

        own = mdl_rank * row_dev
        normed = rms_scale(rows_in, attn_gain).astype(BF16)
        own_normed = lax.dynamic_slice_in_dim(normed, own, row_dev)
        compressed = jnp.dot(own_normed, w_kv_down, preferred_element_type=F32)
        latent = rms_scale(compressed[:, :LATENT], latent_gain).astype(BF16)
        key_rope = turned(
            compressed[:, LATENT:],
            lax.dynamic_slice_in_dim(cosine, own, row_dev),
            lax.dynamic_slice_in_dim(sine, own, row_dev),
        ).astype(BF16)
        keys = lax.all_gather(
            jnp.concatenate([latent, key_rope], axis=1), ("tok", "mdl"), axis=0, tiled=True
        )
        queries = jnp.dot(normed, w_query, preferred_element_type=F32)
        keys = lax.dynamic_slice_in_dim(keys, window, span)
        partial = attend(
            queries, keys[:, :LATENT], keys[:, LATENT:], w_kv_up, w_out, cosine, sine, low, high
        )
        mixed = lax.psum_scatter(partial, "mdl", scatter_dimension=0, tiled=True)
        own_input = lax.dynamic_slice_in_dim(rows_in, own, row_dev)
        residual = (own_input.astype(F32) + mixed.astype(F32)).astype(BF16)
        normed_ffn = rms_scale(residual, ffn_gain).astype(BF16)
        all_rows = lax.all_gather(normed_ffn, ("tok", "mdl"), axis=0, tiled=True)

        group_rows = lax.dynamic_slice_in_dim(all_rows, query_start, tok_dev)
        shared_act = silu_mul(
            jnp.dot(group_rows, w_shared_gate, preferred_element_type=F32),
            jnp.dot(group_rows, w_shared_up, preferred_element_type=F32),
        ).astype(BF16)
        shared_part = jnp.dot(shared_act, w_shared_down, preferred_element_type=F32)
        outgoing = jnp.zeros((pack, model_width), F32)
        for local in range(expert_dev):
            expert = (tok_rank * n_mdl + mdl_rank) * expert_dev + local
            row_weight = lax.dynamic_slice_in_dim(all_combining, expert, 1, axis=1)
            act = silu_mul(
                jnp.dot(all_rows, w_expert_gate[local], preferred_element_type=F32),
                jnp.dot(all_rows, w_expert_up[local], preferred_element_type=F32),
            )
            act = (act * row_weight).astype(BF16)
            outgoing += jnp.dot(act, w_expert_down[local], preferred_element_type=F32)
        group_sum = lax.dynamic_slice_in_dim(outgoing, query_start, tok_dev) + shared_part
        outgoing = lax.dynamic_update_slice_in_dim(outgoing, group_sum, query_start, 0)
        summed = lax.psum_scatter(
            outgoing.astype(BF16), ("tok", "mdl"), scatter_dimension=0, tiled=True
        )
        results.append((residual.astype(F32) + summed.astype(F32)).astype(BF16))
    return jnp.stack(results)


def solution(mesh):
    in_specs = (
        P(None, "tok", None),
        P(),
        P(None, ("tok", "mdl"), None),
        P(None, ("tok", "mdl"), None),
        P(),
        P(None, "mdl"),
        P(),
        P(),
        P(None, "mdl"),
        P("mdl", None),
        P(),
        P(None, "mdl"),
        P(None, "mdl"),
        P("mdl", None),
        P(("tok", "mdl"), None, None),
        P(("tok", "mdl"), None, None),
        P(("tok", "mdl"), None, None),
    )
    out_specs = P("section", ("tok", "mdl"), None)
    return jax.shard_map(shards, mesh=mesh, in_specs=in_specs, out_specs=out_specs, check_vma=False)
```

```python
import math

import jax
import jax.numpy as jnp
from jax import lax
from jax.experimental import pallas as pl
from jax.experimental.pallas import tpu as pltpu
from jax.sharding import PartitionSpec as P

NOPE = 128
ROPE = 64
VDIM = 128
LATENT = 512
SEGS = 4
EPS = 1e-06
BF16 = jnp.bfloat16
F32 = jnp.float32


def rms_scale(values, gain_vec):
    values = values.astype(F32)
    return values * lax.rsqrt(jnp.mean(values * values, axis=-1, keepdims=True) + EPS) * gain_vec


def rotary_tables(positions):
    half_width = ROPE // 2
    frequency = 10000.0 ** (-jnp.arange(half_width, dtype=F32) / half_width)
    angles = positions.astype(F32)[:, None] * frequency[None, :]
    cosine = jnp.cos(angles)
    sine = jnp.sin(angles)
    return jnp.concatenate([cosine, cosine], axis=1), jnp.concatenate([-sine, sine], axis=1)


def turned(values, cosine, sine):
    half_width = values.shape[-1] // 2
    swapped = jnp.concatenate([values[:, half_width:], values[:, :half_width]], axis=1)
    return values * cosine + swapped * sine


def silu_mul(gate, up):
    return gate / (1.0 + jnp.exp(-gate)) * up


def layer_kernel(
    normed_ref, own_lat_ref, cos_ref, sin_ref, low_ref, high_ref, input_ref, gain_ref, combine_ref,
    wq_hbm, wkv_hbm, wo_hbm, sg_hbm, su_hbm, sd_hbm, eg_hbm, eu_hbm, ed_hbm,
    out_ref,
    wq, wkv, wo, sg, su, sd, eg, eu, ed,
    keys, att, rows, act, shared_act, partial, core_in, y_out, y_in, ring_out, ring_in, own_sum, residual,
    w_sem, lat_s, lat_r, latc_s, latc_r, zf_s, zf_r, yf_s, yf_r, cf_s, cf_r,
    rc_s, rc_r, ry_s, ry_r, rz_s, rz_r,
):
    n_tok = lax.axis_size("tok")
    n_mdl = lax.axis_size("mdl")
    n_y = n_mdl // 2
    section = lax.axis_index("section")
    t = lax.axis_index("tok")
    m = lax.axis_index("mdl")
    y, c = m // 2, m % 2
    tok_dev, width = normed_ref.shape
    row_dev = tok_dev // n_mdl
    half = tok_dev // 2
    back = keys.shape[0] // tok_dev - 1
    heads = wo.shape[0] // VDIM
    experts = n_tok * n_mdl
    mesh_id = pl.DeviceIdType.MESH
    sibling = (section, t, y * 2 + 1 - c)

    def tok_peer(step):
        return (section, lax.rem(t + step + n_tok, n_tok), m)

    def rank_y(step):
        return lax.rem(y + step + n_y, n_y) * 2 + c

    def y_peer(step):
        return (section, t, rank_y(step))

    def at_rank(rank):
        return pl.ds(pl.multiple_of(rank * row_dev, row_dev), row_dev)

    def remote(source, target, send_sem, recv_sem, device):
        return pltpu.make_async_remote_copy(
            src_ref=source, dst_ref=target, send_sem=send_sem, recv_sem=recv_sem,
            device_id=device, device_id_type=mesh_id,
        )

    loads = [
        pltpu.make_async_copy(src, dst, w_sem.at[i])
        for i, (src, dst) in enumerate(
            [(wq_hbm, wq), (wkv_hbm, wkv), (wo_hbm, wo), (sg_hbm, sg), (su_hbm, su), (sd_hbm, sd),
             (eg_hbm.at[0], eg), (eu_hbm.at[0], eu), (ed_hbm.at[0], ed)]
        )
    ]
    for load in loads:
        load.start()

    barrier = pltpu.get_barrier_semaphore()
    for step in range(1, back + 1):
        pl.semaphore_signal(barrier, inc=1, device_id=tok_peer(-step), device_id_type=mesh_id)
    pl.semaphore_signal(barrier, inc=1, device_id=sibling, device_id_type=mesh_id)
    for step in range(1, n_y):
        pl.semaphore_signal(barrier, inc=1, device_id=y_peer(-step), device_id_type=mesh_id)
    pl.semaphore_wait(barrier, back + n_y)

    def key_rows(step, core):
        return keys.at[pl.ds(pl.multiple_of(step * tok_dev + core * half, half), half)]

    def lat_copy(step):
        return remote(own_lat_ref, key_rows(step, c), lat_s.at[step], lat_r.at[step], tok_peer(step))

    def lat_core_copy(step):
        source = own_lat_ref if step == 0 else key_rows(step, c)
        return remote(source, key_rows(step, c), latc_s.at[step], latc_r.at[step], sibling)

    for step in range(back, 0, -1):
        lat_copy(step).start()
    lat_core_copy(0).start()
    keys[pl.ds(pl.multiple_of(c * half, half), half), :] = own_lat_ref[...]
    loads[0].wait()
    queries = jnp.dot(normed_ref[...], wq[...], preferred_element_type=F32)
    for step in range(1, back + 1):
        lat_copy(step).wait_recv()
        lat_core_copy(step).start()
    for step in range(back + 1):
        lat_core_copy(step).wait_recv()
    loads[1].wait()

    qk = NOPE + ROPE
    span = keys.shape[0]
    column = lax.broadcasted_iota(jnp.int32, (tok_dev, span), 1)
    key_index = t * tok_dev + column
    for step in range(1, back + 1):
        key_index = key_index - jnp.where(column >= step * tok_dev, 2 * tok_dev, 0)
    allowed = (key_index >= low_ref[...]) & (key_index <= high_ref[...])
    contract = (((1,), (1,)), ((), ()))
    cosine, sine = cos_ref[...], sin_ref[...]
    scale = 1.0 / math.sqrt(qk)
    for h in range(heads):
        kv = jnp.dot(
            keys[:, :LATENT], wkv[:, h * (NOPE + VDIM) : (h + 1) * (NOPE + VDIM)],
            preferred_element_type=F32,
        ).astype(BF16)
        q_nope = queries[:, h * qk : h * qk + NOPE].astype(BF16)
        q_rope = turned(queries[:, h * qk + NOPE : (h + 1) * qk], cosine, sine).astype(BF16)
        scores = lax.dot_general(q_nope, kv[:, :NOPE], contract, preferred_element_type=F32)
        scores += lax.dot_general(q_rope, keys[:, LATENT:], contract, preferred_element_type=F32)
        scores = jnp.where(allowed, scores * scale, -1e30)
        top = jnp.max(scores, axis=1, keepdims=True)
        weights = jnp.where(allowed, jnp.exp(scores - top), 0.0)
        total = jnp.sum(weights, axis=1, keepdims=True)
        summed = jnp.dot(weights.astype(BF16), kv[:, NOPE:], preferred_element_type=F32)
        att[:, h * VDIM : (h + 1) * VDIM] = (summed / total).astype(BF16)
    loads[2].wait()

    chunk = 512

    def chunk_of(i, size):
        return pl.ds(pl.multiple_of(i * size, size), size)

    @pl.loop(0, width // chunk)
    def _(i):
        partial[n_tok, :, chunk_of(i, chunk)] = jnp.dot(
            att[...], wo[:, chunk_of(i, chunk)], preferred_element_type=F32
        ).astype(BF16)

    def core_copy(k, j):
        other = lax.rem(y + j, n_y) * 2 + 1 - c
        return remote(
            partial.at[k, at_rank(other)], core_in.at[k, j], rc_s.at[k, j], rc_r.at[k, j], sibling
        )

    def y_copy(k, j):
        return remote(
            y_out.at[k, j - 1], y_in.at[k, j - 1], ry_s.at[k, j], ry_r.at[k, j], y_peer(j)
        )

    def start_core(k):
        for j in range(n_y):
            core_copy(k, j).start()

    def core_to_y(k):
        for j in range(n_y):
            core_copy(k, j).wait_recv()
        for j in range(1, n_y):
            y_out[k, j - 1] = (
                partial[k, at_rank(rank_y(j)), :].astype(F32) + core_in[k, j].astype(F32)
            ).astype(BF16)
            y_copy(k, j).start()

    def y_total(k):
        for j in range(1, n_y):
            y_copy(k, j).wait_recv()
        total = partial[k, at_rank(m), :].astype(F32) + core_in[k, 0].astype(F32)
        for j in range(1, n_y):
            total += y_in[k, j - 1].astype(F32)
        return total

    start_core(n_tok)
    core_to_y(n_tok)
    res = (input_ref[...].astype(F32) + y_total(n_tok)).astype(BF16)
    residual[...] = res
    rows[0, at_rank(m), :width] = rms_scale(res, gain_ref[...]).astype(BF16)
    combine = combine_ref[...]
    high_part = combine.astype(BF16)
    extra = combine.shape[1]
    rows[0, at_rank(m), width : width + extra] = high_part
    rows[0, at_rank(m), width + extra :] = (combine - high_part.astype(F32)).astype(BF16)

    def z_row_copy(k):
        return remote(
            rows.at[k, at_rank(m)], rows.at[k + 1, at_rank(m)], zf_s.at[k], zf_r.at[k], tok_peer(1)
        )

    def y_row_copy(k, j):
        place = rows.at[k, at_rank(m)]
        return remote(place, place, yf_s.at[k, j], yf_r.at[k, j], y_peer(j))

    def core_row_copy(k, j):
        place = rows.at[k, at_rank(rank_y(-j))]
        return remote(place, place, cf_s.at[k, j], cf_r.at[k, j], sibling)

    def forward(k):
        for j in range(1, n_y):
            y_row_copy(k, j).start()
        core_row_copy(k, 0).start()

    def forward_core(k):
        for j in range(1, n_y):
            y_row_copy(k, j).wait_recv()
            core_row_copy(k, j).start()

    def ring_copy(k):
        return remote(ring_out.at[k], ring_in.at[k], rz_s.at[k], rz_r.at[k], tok_peer(1))

    def to_ring(k):
        total = y_total(k)

        @pl.when(k == 0)
        def _():
            own_sum[...] = total

        @pl.when(k == 1)
        def _():
            ring_out[k] = total.astype(BF16)
            ring_copy(k).start()

        @pl.when(k >= 2)
        def _():
            ring_copy(k - 1).wait_recv()
            ring_out[k] = (total + ring_in[k - 1].astype(F32)).astype(BF16)
            ring_copy(k).start()

    z_row_copy(0).start()
    forward(0)
    forward_core(0)
    for load in loads[3:]:
        load.wait()

    block = 256
    expert = t * n_mdl + m
    lane = lax.broadcasted_iota(jnp.int32, (tok_dev, 2 * extra), 1)
    mine = (lane == expert) | (lane == expert + extra)

    @pl.loop(0, n_tok)
    def _(k):
        for j in range(n_y):
            core_row_copy(k, j).wait_recv()

        @pl.when(k + 1 < n_tok)
        def _():
            z_row_copy(k).wait_recv()

            @pl.when(k + 2 < n_tok)
            def _():
                z_row_copy(k + 1).start()

            forward(k + 1)

        row_weight = jnp.sum(
            jnp.where(mine, rows[k, :, width:].astype(F32), 0.0), axis=1, keepdims=True
        )

        @pl.loop(0, eg.shape[1] // block)
        def _(i):
            group = rows[k, :, :width]
            gate = jnp.dot(group, eg[:, chunk_of(i, block)], preferred_element_type=F32)
            up = jnp.dot(group, eu[:, chunk_of(i, block)], preferred_element_type=F32)
            act[:, chunk_of(i, block)] = (silu_mul(gate, up) * row_weight).astype(BF16)

        @pl.when(k == 0)
        def _():
            @pl.loop(0, sg.shape[1] // block)
            def _(i):
                group = rows[0, :, :width]
                gate = jnp.dot(group, sg[:, chunk_of(i, block)], preferred_element_type=F32)
                up = jnp.dot(group, su[:, chunk_of(i, block)], preferred_element_type=F32)
                shared_act[:, chunk_of(i, block)] = silu_mul(gate, up).astype(BF16)

            @pl.loop(0, width // chunk)
            def _(i):
                partial[k, :, chunk_of(i, chunk)] = (
                    jnp.dot(act[...], ed[:, chunk_of(i, chunk)], preferred_element_type=F32)
                    + jnp.dot(shared_act[...], sd[:, chunk_of(i, chunk)], preferred_element_type=F32)
                ).astype(BF16)

        @pl.when(k > 0)
        def _():
            @pl.loop(0, width // chunk)
            def _(i):
                partial[k, :, chunk_of(i, chunk)] = jnp.dot(
                    act[...], ed[:, chunk_of(i, chunk)], preferred_element_type=F32
                ).astype(BF16)

        start_core(k)

        @pl.when(k >= 1)
        def _():
            to_ring(k - 1)

        @pl.when(k + 1 < n_tok)
        def _():
            forward_core(k + 1)

        core_to_y(k)

    to_ring(jnp.int32(n_tok - 1))
    ring_copy(n_tok - 1).wait_recv()
    out_ref[...] = (
        residual[...].astype(F32) + own_sum[...] + ring_in[n_tok - 1].astype(F32)
    ).astype(BF16)

    for step in range(1, back + 1):
        lat_copy(step).wait_send()
    for step in range(back + 1):
        lat_core_copy(step).wait_send()

    @pl.loop(0, n_tok + 1)
    def _(k):
        for j in range(n_y):
            core_copy(k, j).wait_send()
        for j in range(1, n_y):
            y_copy(k, j).wait_send()

    @pl.loop(0, n_tok)
    def _(k):
        for j in range(n_y):
            core_row_copy(k, j).wait_send()
        for j in range(1, n_y):
            y_row_copy(k, j).wait_send()

    @pl.loop(0, n_tok - 1)
    def _(k):
        z_row_copy(k).wait_send()
        ring_copy(k + 1).wait_send()


def shards(
    layer_input, segment_ids, route_ids, route_weights, attn_gain, w_query, w_kv_down, latent_gain,
    w_kv_up, w_out, ffn_gain, w_shared_gate, w_shared_up, w_shared_down, w_expert_gate, w_expert_up,
    w_expert_down,
):
    n_tok = lax.axis_size("tok")
    n_mdl = lax.axis_size("mdl")
    n_y = n_mdl // 2
    batch = lax.axis_index("section")
    tok_rank = lax.axis_index("tok")
    mdl_rank = lax.axis_index("mdl")
    micro_count, tok_dev, width = layer_input.shape
    assert micro_count == lax.axis_size("section") and w_expert_gate.shape[0] == 1
    row_dev = tok_dev // n_mdl
    half = tok_dev // 2
    pack = segment_ids.shape[1]
    expert_total = n_tok * n_mdl
    back = min(n_tok - 1, -(-(pack // 2) // tok_dev))
    rows_in = lax.dynamic_index_in_dim(layer_input, batch, 0, keepdims=False)
    segment_row = lax.dynamic_index_in_dim(segment_ids, batch, 0, keepdims=False)
    chosen = lax.dynamic_index_in_dim(route_ids, batch, 0, keepdims=False)
    chosen_weights = lax.dynamic_index_in_dim(route_weights, batch, 0, keepdims=False)
    extra = -(-expert_total // 128) * 128
    labels = jnp.arange(extra, dtype=jnp.int32)
    combining = jnp.sum(
        jnp.where(chosen[:, :, None] == labels, chosen_weights[:, :, None], 0.0), axis=1
    )
    query_start = tok_rank * tok_dev
    query_seg = lax.dynamic_slice_in_dim(segment_row, query_start, tok_dev)
    firsts = jnp.sum((segment_row[None, :] < query_seg[:, None]).astype(jnp.int32), axis=1)
    query_index = query_start + jnp.arange(tok_dev, dtype=jnp.int32)
    cosine, sine = rotary_tables(query_index - firsts)
    own = mdl_rank * row_dev
    lead = (mdl_rank % 2) * half
    normed = rms_scale(rows_in, attn_gain).astype(BF16)
    half_normed = lax.dynamic_slice_in_dim(normed, lead, half)
    compressed = jnp.dot(half_normed, w_kv_down, preferred_element_type=F32)
    latent = rms_scale(compressed[:, :LATENT], latent_gain).astype(BF16)
    key_rope = turned(
        compressed[:, LATENT:],
        lax.dynamic_slice_in_dim(cosine, lead, half),
        lax.dynamic_slice_in_dim(sine, lead, half),
    ).astype(BF16)
    own_lat = jnp.concatenate([latent, key_rope], axis=1)
    own_input = lax.dynamic_slice_in_dim(rows_in, own, row_dev)
    inputs = [
        normed, own_lat, cosine, sine, firsts[:, None], query_index[:, None], own_input,
        ffn_gain[None, :], combining,
    ]
    weights = [
        w_query, w_kv_up, w_out, w_shared_gate, w_shared_up, w_shared_down, w_expert_gate,
        w_expert_up, w_expert_down,
    ]
    held = [pltpu.VMEM(w.shape[-2:], BF16) for w in weights]
    dma = pltpu.SemaphoreType.DMA
    result = pl.pallas_call(
        layer_kernel,
        out_shape=jax.ShapeDtypeStruct((row_dev, width), BF16),
        in_specs=[pl.BlockSpec(memory_space=pltpu.VMEM)] * len(inputs)
        + [pl.BlockSpec(memory_space=pl.ANY)] * len(weights),
        out_specs=pl.BlockSpec(memory_space=pltpu.VMEM),
        scratch_shapes=held
        + [
            pltpu.VMEM(((back + 1) * tok_dev, LATENT + ROPE), BF16),
            pltpu.VMEM((tok_dev, w_out.shape[0]), BF16),
            pltpu.VMEM((n_tok, tok_dev, width + 2 * extra), BF16),
            pltpu.VMEM((tok_dev, w_expert_gate.shape[2]), BF16),
            pltpu.VMEM((tok_dev, w_shared_gate.shape[1]), BF16),
            pltpu.VMEM((n_tok + 1, tok_dev, width), BF16),
            pltpu.VMEM((n_tok + 1, n_y, row_dev, width), BF16),
            pltpu.VMEM((n_tok + 1, n_y - 1, row_dev, width), BF16),
            pltpu.VMEM((n_tok + 1, n_y - 1, row_dev, width), BF16),
            pltpu.VMEM((n_tok, row_dev, width), BF16),
            pltpu.VMEM((n_tok, row_dev, width), BF16),
            pltpu.VMEM((row_dev, width), F32),
            pltpu.VMEM((row_dev, width), BF16),
            dma((len(weights),)),
        ]
        + [dma((back + 1,))] * 4
        + [dma((n_tok,))] * 2
        + [dma((n_tok, n_y))] * 4
        + [dma((n_tok + 1, n_y))] * 4
        + [dma((n_tok,))] * 2,
        compiler_params=pltpu.CompilerParams(
            collective_id=0, has_side_effects=True, vmem_limit_bytes=60 * 2**20
        ),
        cost_estimate=pl.CostEstimate(
            flops=14 * 10**9, bytes_accessed=25 * 10**6, transcendentals=2 * 10**6
        ),
    )(*inputs, *weights)
    return result[None]


def solution(mesh):
    in_specs = (
        P(None, "tok", None),
        P(),
        P(None, ("tok", "mdl"), None),
        P(None, ("tok", "mdl"), None),
        P(),
        P(None, "mdl"),
        P(),
        P(),
        P(None, "mdl"),
        P("mdl", None),
        P(),
        P(None, "mdl"),
        P(None, "mdl"),
        P("mdl", None),
        P(("tok", "mdl"), None, None),
        P(("tok", "mdl"), None, None),
        P(("tok", "mdl"), None, None),
    )
    out_specs = P("section", ("tok", "mdl"), None)
    return jax.shard_map(shards, mesh=mesh, in_specs=in_specs, out_specs=out_specs, check_vma=False)
```

```python
import math

import jax
import jax.numpy as jnp
from jax import lax
from jax.experimental import pallas as pl
from jax.experimental.pallas import tpu as pltpu
from jax.sharding import PartitionSpec as P

NOPE = 128
ROPE = 64
VDIM = 128
LATENT = 512
SEGS = 4
EPS = 1e-06
BF16 = jnp.bfloat16
F32 = jnp.float32


def rms_scale(values, gain_vec):
    values = values.astype(F32)
    return values * lax.rsqrt(jnp.mean(values * values, axis=-1, keepdims=True) + EPS) * gain_vec


def rotary_tables(positions):
    half_width = ROPE // 2
    lane = jnp.arange(ROPE, dtype=jnp.int32)
    frequency = 10000.0 ** (-(lane % half_width).astype(F32) / half_width)
    angles = positions.astype(F32)[:, None] * frequency[None, :]
    return jnp.cos(angles), jnp.where(lane < half_width, -1.0, 1.0) * jnp.sin(angles)


def turned(values, cosine, sine):
    half_width = values.shape[-1] // 2
    swapped = jnp.concatenate([values[:, half_width:], values[:, :half_width]], axis=1)
    return values * cosine + swapped * sine


def silu_mul(gate, up):
    return gate / (1.0 + jnp.exp(-gate)) * up


def layer_kernel(
    cos_ref, sin_ref, low_ref, attn_gain_ref, lat_gain_ref, gain_ref, combine_ref,
    x_hbm, wd_hbm, wq_hbm, wkv_hbm, wo_hbm, sg_hbm, su_hbm, sd_hbm, eg_hbm, eu_hbm, ed_hbm,
    out_ref,
    x_in, normed, wd, wq, wkv, wo, sg, su, sd, eg, eu, ed,
    keys, att, rows, act, shared_act, partial, core_in, y_out, y_in, ring_out, ring_in, residual,
    w_sem, lat_s, lat_r, latc_s, latc_r, zf_s, zf_r, yf_s, yf_r, cf_s, cf_r,
    rc_s, rc_r, ry_s, ry_r, rz_s, rz_r,
):
    n_tok = lax.axis_size("tok")
    n_mdl = lax.axis_size("mdl")
    n_y = n_mdl // 2
    section = lax.axis_index("section")
    t = lax.axis_index("tok")
    m = lax.axis_index("mdl")
    y, c = m // 2, m % 2
    tok_dev, width = x_in.shape
    row_dev = tok_dev // n_mdl
    half = tok_dev // 2
    back = keys.shape[0] // tok_dev - 1
    heads = wo.shape[0] // VDIM
    experts = n_tok * n_mdl
    mesh_id = pl.DeviceIdType.MESH
    sibling = (section, t, y * 2 + 1 - c)

    def tok_peer(step):
        return (section, lax.rem(t + step + n_tok, n_tok), m)

    def rank_y(step):
        return lax.rem(y + step + n_y, n_y) * 2 + c

    def y_peer(step):
        return (section, t, rank_y(step))

    def at_rank(rank):
        return pl.ds(pl.multiple_of(rank * row_dev, row_dev), row_dev)

    def remote(source, target, send_sem, recv_sem, device):
        return pltpu.make_async_remote_copy(
            src_ref=source, dst_ref=target, send_sem=send_sem, recv_sem=recv_sem,
            device_id=device, device_id_type=mesh_id,
        )

    loads = [
        pltpu.make_async_copy(src, dst, w_sem.at[i])
        for i, (src, dst) in enumerate(
            [(x_hbm.at[section], x_in), (wd_hbm, wd), (wq_hbm, wq), (wkv_hbm, wkv), (wo_hbm, wo), (sg_hbm, sg), (su_hbm, su), (sd_hbm, sd),
             (eg_hbm.at[0], eg), (eu_hbm.at[0], eu), (ed_hbm.at[0], ed)]
        )
    ]
    for load in loads:
        load.start()

    barrier = pltpu.get_barrier_semaphore()
    pl.semaphore_signal(barrier, inc=1, device_id=tok_peer(-1), device_id_type=mesh_id)
    pl.semaphore_signal(barrier, inc=1, device_id=sibling, device_id_type=mesh_id)
    for step in range(1, n_y):
        pl.semaphore_signal(barrier, inc=1, device_id=y_peer(-step), device_id_type=mesh_id)
    loads[0].wait()
    normed[...] = rms_scale(x_in[...], attn_gain_ref[...]).astype(BF16)
    lead = pl.ds(pl.multiple_of(c * half, half), half)
    loads[1].wait()
    compressed = jnp.dot(normed[lead, :], wd[...], preferred_element_type=F32)
    keys[lead, :LATENT] = rms_scale(compressed[:, :LATENT], lat_gain_ref[...]).astype(BF16)
    keys[lead, LATENT:] = turned(
        compressed[:, LATENT:], cos_ref[lead, :], sin_ref[lead, :]
    ).astype(BF16)
    pl.semaphore_wait(barrier, 1 + n_y)

    def key_rows(step, core):
        return keys.at[pl.ds(pl.multiple_of(step * tok_dev + core * half, half), half)]

    def lat_copy(step):
        return remote(
            key_rows(step - 1, c), key_rows(step, c), lat_s.at[step], lat_r.at[step], tok_peer(1)
        )

    def lat_core_copy(step):
        place = key_rows(step, c)
        return remote(place, place, latc_s.at[step], latc_r.at[step], sibling)

    lat_copy(1).start()
    lat_core_copy(0).start()
    loads[2].wait()
    queries = jnp.dot(normed[...], wq[...], preferred_element_type=F32)
    for step in range(1, back + 1):
        lat_copy(step).wait_recv()
        if step < back:
            lat_copy(step + 1).start()
        lat_core_copy(step).start()
    for step in range(back + 1):
        lat_core_copy(step).wait_recv()
    loads[3].wait()

    qk = NOPE + ROPE
    span = keys.shape[0]
    column = lax.broadcasted_iota(jnp.int32, (tok_dev, span), 1)
    key_index = t * tok_dev + column
    query_index = t * tok_dev + lax.broadcasted_iota(jnp.int32, (tok_dev, span), 0)
    for step in range(1, back + 1):
        key_index = key_index - jnp.where(column >= step * tok_dev, 2 * tok_dev, 0)
    allowed = (key_index >= low_ref[...]) & (key_index <= query_index)
    contract = (((1,), (1,)), ((), ()))
    cosine, sine = cos_ref[...], sin_ref[...]
    scale = 1.0 / math.sqrt(qk)
    for h in range(heads):
        kv = jnp.dot(
            keys[:, :LATENT], wkv[:, h * (NOPE + VDIM) : (h + 1) * (NOPE + VDIM)],
            preferred_element_type=F32,
        ).astype(BF16)
        q_nope = queries[:, h * qk : h * qk + NOPE].astype(BF16)
        q_rope = turned(queries[:, h * qk + NOPE : (h + 1) * qk], cosine, sine).astype(BF16)
        scores = lax.dot_general(q_nope, kv[:, :NOPE], contract, preferred_element_type=F32)
        scores += lax.dot_general(q_rope, keys[:, LATENT:], contract, preferred_element_type=F32)
        scores = jnp.where(allowed, scores * scale, -1e30)
        top = jnp.max(scores, axis=1, keepdims=True)
        weights = jnp.where(allowed, jnp.exp(scores - top), 0.0)
        total = jnp.sum(weights, axis=1, keepdims=True)
        summed = jnp.dot(weights.astype(BF16), kv[:, NOPE:], preferred_element_type=F32)
        att[:, h * VDIM : (h + 1) * VDIM] = (summed / total).astype(BF16)
    loads[4].wait()

    chunk = 512

    def chunk_of(i, size):
        return pl.ds(pl.multiple_of(i * size, size), size)

    @pl.loop(0, width // chunk)
    def _(i):
        partial[n_tok, :, chunk_of(i, chunk)] = jnp.dot(
            att[...], wo[:, chunk_of(i, chunk)], preferred_element_type=F32
        ).astype(BF16)

    def core_copy(k, j):
        other = lax.rem(y + j, n_y) * 2 + 1 - c
        return remote(
            partial.at[k, at_rank(other)], core_in.at[k, j], rc_s.at[k, j], rc_r.at[k, j], sibling
        )

    def y_copy(k, j):
        return remote(
            y_out.at[k, j - 1], y_in.at[k, j - 1], ry_s.at[k, j], ry_r.at[k, j], y_peer(j)
        )

    def start_core(k):
        for j in range(n_y):
            core_copy(k, j).start()

    def core_to_y(k):
        for j in range(n_y):
            core_copy(k, j).wait_recv()
        for j in range(1, n_y):
            y_out[k, j - 1] = (
                partial[k, at_rank(rank_y(j)), :].astype(F32) + core_in[k, j].astype(F32)
            ).astype(BF16)
            y_copy(k, j).start()

    def y_total(k):
        for j in range(1, n_y):
            y_copy(k, j).wait_recv()
        total = partial[k, at_rank(m), :].astype(F32) + core_in[k, 0].astype(F32)
        for j in range(1, n_y):
            total += y_in[k, j - 1].astype(F32)
        return total

    start_core(n_tok)
    core_to_y(n_tok)
    res = (x_in[at_rank(m), :].astype(F32) + y_total(n_tok)).astype(BF16)
    residual[...] = res
    rows[0, at_rank(m), :width] = rms_scale(res, gain_ref[...]).astype(BF16)
    combine = combine_ref[...]
    high_part = combine.astype(BF16)
    extra = combine.shape[1]
    rows[0, at_rank(m), width : width + extra] = high_part
    rows[0, at_rank(m), width + extra :] = (combine - high_part.astype(F32)).astype(BF16)

    def z_row_copy(k):
        return remote(
            rows.at[k, at_rank(m)], rows.at[k + 1, at_rank(m)], zf_s.at[k], zf_r.at[k], tok_peer(1)
        )

    def y_row_copy(k, j):
        place = rows.at[k, at_rank(m)]
        return remote(place, place, yf_s.at[k, j], yf_r.at[k, j], y_peer(j))

    def core_row_copy(k, j):
        place = rows.at[k, at_rank(rank_y(-j))]
        return remote(place, place, cf_s.at[k, j], cf_r.at[k, j], sibling)

    def forward(k):
        for j in range(1, n_y):
            y_row_copy(k, j).start()
        core_row_copy(k, 0).start()

    def forward_core(k):
        for j in range(1, n_y):
            y_row_copy(k, j).wait_recv()
            core_row_copy(k, j).start()

    def ring_copy(k):
        return remote(ring_out.at[k], ring_in.at[k], rz_s.at[k], rz_r.at[k], tok_peer(1))

    def to_ring(k):
        total = y_total(k)

        @pl.when(k == 1)
        def _():
            ring_out[k] = total.astype(BF16)
            ring_copy(k).start()

        @pl.when(k >= 2)
        def _():
            ring_copy(k - 1).wait_recv()
            ring_out[k] = (total + ring_in[k - 1].astype(F32)).astype(BF16)
            ring_copy(k).start()

    z_row_copy(0).start()
    forward(0)
    forward_core(0)
    for load in loads[5:]:
        load.wait()

    block = 256
    expert = t * n_mdl + m
    lane = lax.broadcasted_iota(jnp.int32, (tok_dev, 2 * extra), 1)
    mine = (lane == expert) | (lane == expert + extra)

    @pl.loop(0, n_tok)
    def _(k):
        for j in range(n_y):
            core_row_copy(k, j).wait_recv()

        @pl.when(k + 1 < n_tok)
        def _():
            z_row_copy(k).wait_recv()

            @pl.when(k + 2 < n_tok)
            def _():
                z_row_copy(k + 1).start()

            forward(k + 1)

        row_weight = jnp.sum(
            jnp.where(mine, rows[k, :, width:].astype(F32), 0.0), axis=1, keepdims=True
        )

        @pl.loop(0, eg.shape[1] // block)
        def _(i):
            group = rows[k, :, :width]
            gate = jnp.dot(group, eg[:, chunk_of(i, block)], preferred_element_type=F32)
            up = jnp.dot(group, eu[:, chunk_of(i, block)], preferred_element_type=F32)
            act[:, chunk_of(i, block)] = (silu_mul(gate, up) * row_weight).astype(BF16)

        @pl.when(k == 0)
        def _():
            @pl.loop(0, sg.shape[1] // block)
            def _(i):
                group = rows[0, :, :width]
                gate = jnp.dot(group, sg[:, chunk_of(i, block)], preferred_element_type=F32)
                up = jnp.dot(group, su[:, chunk_of(i, block)], preferred_element_type=F32)
                shared_act[:, chunk_of(i, block)] = silu_mul(gate, up).astype(BF16)

            @pl.loop(0, width // chunk)
            def _(i):
                partial[k, :, chunk_of(i, chunk)] = (
                    jnp.dot(act[...], ed[:, chunk_of(i, chunk)], preferred_element_type=F32)
                    + jnp.dot(shared_act[...], sd[:, chunk_of(i, chunk)], preferred_element_type=F32)
                ).astype(BF16)

        @pl.when(k > 0)
        def _():
            @pl.loop(0, width // chunk)
            def _(i):
                partial[k, :, chunk_of(i, chunk)] = jnp.dot(
                    act[...], ed[:, chunk_of(i, chunk)], preferred_element_type=F32
                ).astype(BF16)

        start_core(k)

        @pl.when(k >= 2)
        def _():
            to_ring(k - 1)

        @pl.when(k + 1 < n_tok)
        def _():
            forward_core(k + 1)

        @pl.when(k >= 1)
        def _():
            core_to_y(k)

    core_to_y(0)
    to_ring(jnp.int32(n_tok - 1))
    own_sum = y_total(0)
    ring_copy(n_tok - 1).wait_recv()
    out_ref[...] = (
        residual[...].astype(F32) + own_sum + ring_in[n_tok - 1].astype(F32)
    ).astype(BF16)

    for step in range(1, back + 1):
        lat_copy(step).wait_send()
    for step in range(back + 1):
        lat_core_copy(step).wait_send()

    @pl.loop(0, n_tok + 1)
    def _(k):
        for j in range(n_y):
            core_copy(k, j).wait_send()
        for j in range(1, n_y):
            y_copy(k, j).wait_send()

    @pl.loop(0, n_tok)
    def _(k):
        for j in range(n_y):
            core_row_copy(k, j).wait_send()
        for j in range(1, n_y):
            y_row_copy(k, j).wait_send()

    @pl.loop(0, n_tok - 1)
    def _(k):
        z_row_copy(k).wait_send()
        ring_copy(k + 1).wait_send()


def shards(
    layer_input, segment_ids, route_ids, route_weights, attn_gain, w_query, w_kv_down, latent_gain,
    w_kv_up, w_out, ffn_gain, w_shared_gate, w_shared_up, w_shared_down, w_expert_gate, w_expert_up,
    w_expert_down,
):
    n_tok = lax.axis_size("tok")
    n_mdl = lax.axis_size("mdl")
    n_y = n_mdl // 2
    batch = lax.axis_index("section")
    tok_rank = lax.axis_index("tok")
    micro_count, tok_dev, width = layer_input.shape
    assert micro_count == lax.axis_size("section") and w_expert_gate.shape[0] == 1
    row_dev = tok_dev // n_mdl
    pack = segment_ids.shape[1]
    expert_total = n_tok * n_mdl
    back = min(n_tok - 1, -(-(pack // 2) // tok_dev))
    segment_row = lax.dynamic_index_in_dim(segment_ids, batch, 0, keepdims=False)
    chosen = lax.dynamic_index_in_dim(route_ids, batch, 0, keepdims=False)
    chosen_weights = lax.dynamic_index_in_dim(route_weights, batch, 0, keepdims=False)
    extra = -(-expert_total // 128) * 128
    labels = jnp.arange(extra, dtype=jnp.int32)
    combining = jnp.sum(
        jnp.where(chosen[:, :, None] == labels, chosen_weights[:, :, None], 0.0), axis=1
    )
    query_start = tok_rank * tok_dev
    query_seg = lax.dynamic_slice_in_dim(segment_row, query_start, tok_dev)
    firsts = jnp.sum((segment_row[None, :] < query_seg[:, None]).astype(jnp.int32), axis=1)
    query_index = query_start + jnp.arange(tok_dev, dtype=jnp.int32)
    cosine, sine = rotary_tables(query_index - firsts)
    inputs = [
        cosine, sine, firsts[:, None], attn_gain[None, :], latent_gain[None, :], ffn_gain[None, :],
        combining,
    ]
    weights = [
        layer_input, w_kv_down, w_query, w_kv_up, w_out, w_shared_gate, w_shared_up, w_shared_down, w_expert_gate,
        w_expert_up, w_expert_down,
    ]
    held = [pltpu.VMEM((tok_dev, width), BF16)] * 2
    held += [pltpu.VMEM(w.shape[-2:], BF16) for w in weights[1:]]
    dma = pltpu.SemaphoreType.DMA
    result = pl.pallas_call(
        layer_kernel,
        out_shape=jax.ShapeDtypeStruct((row_dev, width), BF16),
        in_specs=[pl.BlockSpec(memory_space=pltpu.VMEM)] * len(inputs)
        + [pl.BlockSpec(memory_space=pl.ANY)] * len(weights),
        out_specs=pl.BlockSpec(memory_space=pltpu.VMEM),
        scratch_shapes=held
        + [
            pltpu.VMEM(((back + 1) * tok_dev, LATENT + ROPE), BF16),
            pltpu.VMEM((tok_dev, w_out.shape[0]), BF16),
            pltpu.VMEM((n_tok, tok_dev, width + 2 * extra), BF16),
            pltpu.VMEM((tok_dev, w_expert_gate.shape[2]), BF16),
            pltpu.VMEM((tok_dev, w_shared_gate.shape[1]), BF16),
            pltpu.VMEM((n_tok + 1, tok_dev, width), BF16),
            pltpu.VMEM((n_tok + 1, n_y, row_dev, width), BF16),
            pltpu.VMEM((n_tok + 1, n_y - 1, row_dev, width), BF16),
            pltpu.VMEM((n_tok + 1, n_y - 1, row_dev, width), BF16),
            pltpu.VMEM((n_tok, row_dev, width), BF16),
            pltpu.VMEM((n_tok, row_dev, width), BF16),
            pltpu.VMEM((row_dev, width), BF16),
            dma((len(weights),)),
        ]
        + [dma((back + 1,))] * 4
        + [dma((n_tok,))] * 2
        + [dma((n_tok, n_y))] * 4
        + [dma((n_tok + 1, n_y))] * 4
        + [dma((n_tok,))] * 2,
        compiler_params=pltpu.CompilerParams(
            collective_id=0, has_side_effects=True, vmem_limit_bytes=60 * 2**20
        ),
        cost_estimate=pl.CostEstimate(
            flops=14 * 10**9, bytes_accessed=25 * 10**6, transcendentals=2 * 10**6
        ),
    )(*inputs, *weights)
    return result[None]


def solution(mesh):
    in_specs = (
        P(None, "tok", None),
        P(),
        P(None, ("tok", "mdl"), None),
        P(None, ("tok", "mdl"), None),
        P(),
        P(None, "mdl"),
        P(),
        P(),
        P(None, "mdl"),
        P("mdl", None),
        P(),
        P(None, "mdl"),
        P(None, "mdl"),
        P("mdl", None),
        P(("tok", "mdl"), None, None),
        P(("tok", "mdl"), None, None),
        P(("tok", "mdl"), None, None),
    )
    out_specs = P("section", ("tok", "mdl"), None)
    return jax.shard_map(shards, mesh=mesh, in_specs=in_specs, out_specs=out_specs, check_vma=False)
```

```python
import math

import jax
import jax.numpy as jnp
from jax import lax
from jax.experimental import pallas as pl
from jax.experimental.pallas import tpu as pltpu
from jax.sharding import PartitionSpec as P

NOPE = 128
ROPE = 64
VDIM = 128
LATENT = 512
SEGS = 4
EPS = 1e-06
BF16 = jnp.bfloat16
F32 = jnp.float32


def rms_scale(values, gain_vec):
    values = values.astype(F32)
    return values * lax.rsqrt(jnp.mean(values * values, axis=-1, keepdims=True) + EPS) * gain_vec


def rotary_tables(positions):
    half_width = ROPE // 2
    lane = jnp.arange(ROPE, dtype=jnp.int32)
    frequency = 10000.0 ** (-(lane % half_width).astype(F32) / half_width)
    angles = positions.astype(F32)[:, None] * frequency[None, :]
    return jnp.cos(angles), jnp.where(lane < half_width, -1.0, 1.0) * jnp.sin(angles)


def turned(values, cosine, sine):
    half_width = values.shape[-1] // 2
    swapped = jnp.concatenate([values[:, half_width:], values[:, :half_width]], axis=1)
    return values * cosine + swapped * sine


def silu_mul(gate, up):
    return gate / (1.0 + jnp.exp(-gate)) * up


def layer_kernel(
    cos_ref, sin_ref, low_ref, attn_gain_ref, lat_gain_ref, gain_ref, combine_ref,
    x_hbm, wd_hbm, wq_hbm, wkv_hbm, wo_hbm, sg_hbm, su_hbm, sd_hbm, eg_hbm, eu_hbm, ed_hbm,
    out_ref,
    x_in, normed, wd, wq, wkv, wo, sg, su, sd, eg, eu, ed,
    keys, att, rows, act, shared_act, partial, core_in, y_out, y_in, ring_out, ring_in, residual,
    w_sem, lat_s, lat_r, latc_s, latc_r, zf_s, zf_r, yf_s, yf_r, cf_s, cf_r,
    rc_s, rc_r, ry_s, ry_r, rz_s, rz_r,
):
    n_tok = lax.axis_size("tok")
    n_mdl = lax.axis_size("mdl")
    n_y = n_mdl // 2
    section = lax.axis_index("section")
    t = lax.axis_index("tok")
    m = lax.axis_index("mdl")
    y, c = m // 2, m % 2
    tok_dev, width = x_in.shape
    row_dev = tok_dev // n_mdl
    half = tok_dev // 2
    back = keys.shape[0] // tok_dev - 1
    heads = wo.shape[0] // VDIM
    experts = n_tok * n_mdl
    mesh_id = pl.DeviceIdType.MESH
    sibling = (section, t, y * 2 + 1 - c)

    def tok_peer(step):
        return (section, lax.rem(t + step + n_tok, n_tok), m)

    def rank_y(step):
        return lax.rem(y + step + n_y, n_y) * 2 + c

    def y_peer(step):
        return (section, t, rank_y(step))

    def at_rank(rank):
        return pl.ds(pl.multiple_of(rank * row_dev, row_dev), row_dev)

    def remote(source, target, send_sem, recv_sem, device):
        return pltpu.make_async_remote_copy(
            src_ref=source, dst_ref=target, send_sem=send_sem, recv_sem=recv_sem,
            device_id=device, device_id_type=mesh_id,
        )

    loads = [
        pltpu.make_async_copy(src, dst, w_sem.at[i])
        for i, (src, dst) in enumerate(
            [(x_hbm.at[section], x_in), (wd_hbm, wd), (wq_hbm, wq), (wkv_hbm, wkv), (wo_hbm, wo), (sg_hbm, sg), (su_hbm, su), (sd_hbm, sd),
             (eg_hbm.at[0], eg), (eu_hbm.at[0], eu), (ed_hbm.at[0], ed)]
        )
    ]
    for load in loads:
        load.start()

    barrier = pltpu.get_barrier_semaphore()
    pl.semaphore_signal(barrier, inc=1, device_id=tok_peer(-1), device_id_type=mesh_id)
    pl.semaphore_signal(barrier, inc=1, device_id=sibling, device_id_type=mesh_id)
    for step in range(1, n_y):
        pl.semaphore_signal(barrier, inc=1, device_id=y_peer(-step), device_id_type=mesh_id)
    loads[0].wait()
    normed[...] = rms_scale(x_in[...], attn_gain_ref[...]).astype(BF16)
    lead = pl.ds(pl.multiple_of(c * half, half), half)
    loads[1].wait()
    compressed = lax.dot_general(
        normed[lead, :], wd[...], (((1,), (1,)), ((), ())), preferred_element_type=F32
    )
    keys[lead, :LATENT] = rms_scale(compressed[:, :LATENT], lat_gain_ref[...]).astype(BF16)
    keys[lead, LATENT:] = turned(
        compressed[:, LATENT:], cos_ref[lead, :], sin_ref[lead, :]
    ).astype(BF16)
    pl.semaphore_wait(barrier, 1 + n_y)

    def key_rows(step, core):
        return keys.at[pl.ds(pl.multiple_of(step * tok_dev + core * half, half), half)]

    def lat_copy(step):
        return remote(
            key_rows(step - 1, c), key_rows(step, c), lat_s.at[step], lat_r.at[step], tok_peer(1)
        )

    def lat_core_copy(step):
        place = key_rows(step, c)
        return remote(place, place, latc_s.at[step], latc_r.at[step], sibling)

    lat_copy(1).start()
    lat_core_copy(0).start()
    loads[2].wait()
    queries = jnp.dot(normed[...], wq[...], preferred_element_type=F32)
    for step in range(1, back + 1):
        lat_copy(step).wait_recv()
        if step < back:
            lat_copy(step + 1).start()
        lat_core_copy(step).start()
    for step in range(back + 1):
        lat_core_copy(step).wait_recv()
    loads[3].wait()

    qk = NOPE + ROPE
    span = keys.shape[0]
    column = lax.broadcasted_iota(jnp.int32, (tok_dev, span), 1)
    key_index = t * tok_dev + column
    query_index = t * tok_dev + lax.broadcasted_iota(jnp.int32, (tok_dev, span), 0)
    for step in range(1, back + 1):
        key_index = key_index - jnp.where(column >= step * tok_dev, 2 * tok_dev, 0)
    allowed = (key_index >= low_ref[...]) & (key_index <= query_index)
    contract = (((1,), (1,)), ((), ()))
    cosine, sine = cos_ref[...], sin_ref[...]
    scale = 1.0 / math.sqrt(qk)
    for h in range(heads):
        kv = jnp.dot(
            keys[:, :LATENT], wkv[:, h * (NOPE + VDIM) : (h + 1) * (NOPE + VDIM)],
            preferred_element_type=F32,
        ).astype(BF16)
        q_nope = queries[:, h * qk : h * qk + NOPE].astype(BF16)
        q_rope = turned(queries[:, h * qk + NOPE : (h + 1) * qk], cosine, sine).astype(BF16)
        scores = lax.dot_general(q_nope, kv[:, :NOPE], contract, preferred_element_type=F32)
        scores += lax.dot_general(q_rope, keys[:, LATENT:], contract, preferred_element_type=F32)
        scores = jnp.where(allowed, scores * scale, -1e30)
        top = jnp.max(scores, axis=1, keepdims=True)
        weights = jnp.where(allowed, jnp.exp(scores - top), 0.0)
        total = jnp.sum(weights, axis=1, keepdims=True)
        summed = jnp.dot(weights.astype(BF16), kv[:, NOPE:], preferred_element_type=F32)
        att[:, h * VDIM : (h + 1) * VDIM] = (summed / total).astype(BF16)
    loads[4].wait()

    chunk = 512

    def chunk_of(i, size):
        return pl.ds(pl.multiple_of(i * size, size), size)

    @pl.loop(0, width // chunk)
    def _(i):
        partial[n_tok, :, chunk_of(i, chunk)] = jnp.dot(
            att[...], wo[:, chunk_of(i, chunk)], preferred_element_type=F32
        ).astype(BF16)

    def core_copy(k, j):
        other = lax.rem(y + j, n_y) * 2 + 1 - c
        return remote(
            partial.at[k, at_rank(other)], core_in.at[k, j], rc_s.at[k, j], rc_r.at[k, j], sibling
        )

    def y_copy(k, j):
        return remote(
            y_out.at[k, j - 1], y_in.at[k, j - 1], ry_s.at[k, j], ry_r.at[k, j], y_peer(j)
        )

    def start_core(k):
        for j in range(n_y):
            core_copy(k, j).start()

    def core_to_y(k):
        for j in range(n_y):
            core_copy(k, j).wait_recv()
        for j in range(1, n_y):
            y_out[k, j - 1] = (
                partial[k, at_rank(rank_y(j)), :].astype(F32) + core_in[k, j].astype(F32)
            ).astype(BF16)
            y_copy(k, j).start()

    def y_total(k):
        for j in range(1, n_y):
            y_copy(k, j).wait_recv()
        total = partial[k, at_rank(m), :].astype(F32) + core_in[k, 0].astype(F32)
        for j in range(1, n_y):
            total += y_in[k, j - 1].astype(F32)
        return total

    start_core(n_tok)
    core_to_y(n_tok)
    res = (x_in[at_rank(m), :].astype(F32) + y_total(n_tok)).astype(BF16)
    residual[...] = res
    rows[0, at_rank(m), :width] = rms_scale(res, gain_ref[...]).astype(BF16)
    combine = combine_ref[...]
    high_part = combine.astype(BF16)
    extra = combine.shape[1]
    rows[0, at_rank(m), width : width + extra] = high_part
    rows[0, at_rank(m), width + extra :] = (combine - high_part.astype(F32)).astype(BF16)

    def z_row_copy(k):
        return remote(
            rows.at[k, at_rank(m)], rows.at[k + 1, at_rank(m)], zf_s.at[k], zf_r.at[k], tok_peer(1)
        )

    def y_row_copy(k, j):
        place = rows.at[k, at_rank(m)]
        return remote(place, place, yf_s.at[k, j], yf_r.at[k, j], y_peer(j))

    def core_row_copy(k, j):
        place = rows.at[k, at_rank(rank_y(-j))]
        return remote(place, place, cf_s.at[k, j], cf_r.at[k, j], sibling)

    def forward(k):
        for j in range(1, n_y):
            y_row_copy(k, j).start()
        core_row_copy(k, 0).start()

    def forward_core(k):
        for j in range(1, n_y):
            y_row_copy(k, j).wait_recv()
            core_row_copy(k, j).start()

    def ring_copy(k):
        return remote(ring_out.at[k], ring_in.at[k], rz_s.at[k], rz_r.at[k], tok_peer(1))

    def to_ring(k):
        total = y_total(k)

        @pl.when(k == 1)
        def _():
            ring_out[k] = total.astype(BF16)
            ring_copy(k).start()

        @pl.when(k >= 2)
        def _():
            ring_copy(k - 1).wait_recv()
            ring_out[k] = (total + ring_in[k - 1].astype(F32)).astype(BF16)
            ring_copy(k).start()

    z_row_copy(0).start()
    forward(0)
    forward_core(0)
    for load in loads[5:]:
        load.wait()

    block = 256
    expert = t * n_mdl + m
    lane = lax.broadcasted_iota(jnp.int32, (tok_dev, 2 * extra), 1)
    mine = (lane == expert) | (lane == expert + extra)

    @pl.loop(0, n_tok)
    def _(k):
        for j in range(n_y):
            core_row_copy(k, j).wait_recv()

        @pl.when(k + 1 < n_tok)
        def _():
            z_row_copy(k).wait_recv()

            @pl.when(k + 2 < n_tok)
            def _():
                z_row_copy(k + 1).start()

            forward(k + 1)

        row_weight = jnp.sum(
            jnp.where(mine, rows[k, :, width:].astype(F32), 0.0), axis=1, keepdims=True
        )

        @pl.loop(0, eg.shape[1] // block)
        def _(i):
            group = rows[k, :, :width]
            gate = jnp.dot(group, eg[:, chunk_of(i, block)], preferred_element_type=F32)
            up = jnp.dot(group, eu[:, chunk_of(i, block)], preferred_element_type=F32)
            act[:, chunk_of(i, block)] = (silu_mul(gate, up) * row_weight).astype(BF16)

        @pl.when(k == 0)
        def _():
            @pl.loop(0, sg.shape[1] // block)
            def _(i):
                group = rows[0, :, :width]
                gate = jnp.dot(group, sg[:, chunk_of(i, block)], preferred_element_type=F32)
                up = jnp.dot(group, su[:, chunk_of(i, block)], preferred_element_type=F32)
                shared_act[:, chunk_of(i, block)] = silu_mul(gate, up).astype(BF16)

            @pl.loop(0, width // chunk)
            def _(i):
                partial[k, :, chunk_of(i, chunk)] = (
                    jnp.dot(act[...], ed[:, chunk_of(i, chunk)], preferred_element_type=F32)
                    + jnp.dot(shared_act[...], sd[:, chunk_of(i, chunk)], preferred_element_type=F32)
                ).astype(BF16)

        @pl.when(k > 0)
        def _():
            @pl.loop(0, width // chunk)
            def _(i):
                partial[k, :, chunk_of(i, chunk)] = jnp.dot(
                    act[...], ed[:, chunk_of(i, chunk)], preferred_element_type=F32
                ).astype(BF16)

        start_core(k)

        @pl.when(k + 1 < n_tok)
        def _():
            forward_core(k + 1)

        @pl.when(k >= 1)
        def _():
            core_to_y(k)

        @pl.when(k >= 2)
        def _():
            to_ring(k - 1)

    core_to_y(0)
    to_ring(jnp.int32(n_tok - 1))
    own_sum = y_total(0)
    ring_copy(n_tok - 1).wait_recv()
    out_ref[...] = (
        residual[...].astype(F32) + own_sum + ring_in[n_tok - 1].astype(F32)
    ).astype(BF16)

    for step in range(1, back + 1):
        lat_copy(step).wait_send()
    for step in range(back + 1):
        lat_core_copy(step).wait_send()

    @pl.loop(0, n_tok + 1)
    def _(k):
        for j in range(n_y):
            core_copy(k, j).wait_send()
        for j in range(1, n_y):
            y_copy(k, j).wait_send()

    @pl.loop(0, n_tok)
    def _(k):
        for j in range(n_y):
            core_row_copy(k, j).wait_send()
        for j in range(1, n_y):
            y_row_copy(k, j).wait_send()

    @pl.loop(0, n_tok - 1)
    def _(k):
        z_row_copy(k).wait_send()
        ring_copy(k + 1).wait_send()


def shards(
    layer_input, segment_ids, route_ids, route_weights, attn_gain, w_query, w_kv_down, latent_gain,
    w_kv_up, w_out, ffn_gain, w_shared_gate, w_shared_up, w_shared_down, w_expert_gate, w_expert_up,
    w_expert_down,
):
    n_tok = lax.axis_size("tok")
    n_mdl = lax.axis_size("mdl")
    n_y = n_mdl // 2
    batch = lax.axis_index("section")
    tok_rank = lax.axis_index("tok")
    micro_count, tok_dev, width = layer_input.shape
    assert micro_count == lax.axis_size("section") and w_expert_gate.shape[0] == 1
    row_dev = tok_dev // n_mdl
    pack = segment_ids.shape[1]
    expert_total = n_tok * n_mdl
    back = min(n_tok - 1, -(-(pack // 2) // tok_dev))
    segment_row = lax.dynamic_index_in_dim(segment_ids, batch, 0, keepdims=False)
    chosen = lax.dynamic_index_in_dim(route_ids, batch, 0, keepdims=False)
    chosen_weights = lax.dynamic_index_in_dim(route_weights, batch, 0, keepdims=False)
    extra = -(-expert_total // 128) * 128
    labels = jnp.arange(extra, dtype=jnp.int32)
    combining = jnp.sum(
        jnp.where(chosen[:, :, None] == labels, chosen_weights[:, :, None], 0.0), axis=1
    )
    query_start = tok_rank * tok_dev
    query_seg = lax.dynamic_slice_in_dim(segment_row, query_start, tok_dev)
    firsts = jnp.sum((segment_row[None, :] < query_seg[:, None]).astype(jnp.int32), axis=1)
    query_index = query_start + jnp.arange(tok_dev, dtype=jnp.int32)
    cosine, sine = rotary_tables(query_index - firsts)
    inputs = [
        cosine, sine, firsts[:, None], attn_gain[None, :], latent_gain[None, :], ffn_gain[None, :],
        combining,
    ]
    weights = [
        layer_input, w_kv_down.T, w_query, w_kv_up, w_out, w_shared_gate, w_shared_up, w_shared_down, w_expert_gate,
        w_expert_up, w_expert_down,
    ]
    held = [pltpu.VMEM((tok_dev, width), BF16)] * 2
    held += [pltpu.VMEM(w.shape[-2:], BF16) for w in weights[1:]]
    dma = pltpu.SemaphoreType.DMA
    result = pl.pallas_call(
        layer_kernel,
        out_shape=jax.ShapeDtypeStruct((row_dev, width), BF16),
        in_specs=[pl.BlockSpec(memory_space=pltpu.VMEM)] * len(inputs)
        + [pl.BlockSpec(memory_space=pl.ANY)] * len(weights),
        out_specs=pl.BlockSpec(memory_space=pltpu.VMEM),
        scratch_shapes=held
        + [
            pltpu.VMEM(((back + 1) * tok_dev, LATENT + ROPE), BF16),
            pltpu.VMEM((tok_dev, w_out.shape[0]), BF16),
            pltpu.VMEM((n_tok, tok_dev, width + 2 * extra), BF16),
            pltpu.VMEM((tok_dev, w_expert_gate.shape[2]), BF16),
            pltpu.VMEM((tok_dev, w_shared_gate.shape[1]), BF16),
            pltpu.VMEM((n_tok + 1, tok_dev, width), BF16),
            pltpu.VMEM((n_tok + 1, n_y, row_dev, width), BF16),
            pltpu.VMEM((n_tok + 1, n_y - 1, row_dev, width), BF16),
            pltpu.VMEM((n_tok + 1, n_y - 1, row_dev, width), BF16),
            pltpu.VMEM((n_tok, row_dev, width), BF16),
            pltpu.VMEM((n_tok, row_dev, width), BF16),
            pltpu.VMEM((row_dev, width), BF16),
            dma((len(weights),)),
        ]
        + [dma((back + 1,))] * 4
        + [dma((n_tok,))] * 2
        + [dma((n_tok, n_y))] * 4
        + [dma((n_tok + 1, n_y))] * 4
        + [dma((n_tok,))] * 2,
        compiler_params=pltpu.CompilerParams(
            collective_id=0, has_side_effects=True, vmem_limit_bytes=60 * 2**20
        ),
        cost_estimate=pl.CostEstimate(
            flops=14 * 10**9, bytes_accessed=25 * 10**6, transcendentals=2 * 10**6
        ),
    )(*inputs, *weights)
    return result[None]


def solution(mesh):
    in_specs = (
        P(None, "tok", None),
        P(),
        P(None, ("tok", "mdl"), None),
        P(None, ("tok", "mdl"), None),
        P(),
        P(None, "mdl"),
        P(),
        P(),
        P(None, "mdl"),
        P("mdl", None),
        P(),
        P(None, "mdl"),
        P(None, "mdl"),
        P("mdl", None),
        P(("tok", "mdl"), None, None),
        P(("tok", "mdl"), None, None),
        P(("tok", "mdl"), None, None),
    )
    out_specs = P("section", ("tok", "mdl"), None)
    return jax.shard_map(shards, mesh=mesh, in_specs=in_specs, out_specs=out_specs, check_vma=False)
```
